128 devices in a mesh: tile: 32 (over x, z, core), panel: 4 (over y).
Axes of the slice: x: 4, y: 4, z: 4, core: 2. Of those that a mesh axis runs over, the one named last changes fastest.
Arguments:
- masks: bfloat16 [512, 1024, 1024], P('tile', 'panel'), may hold values from -1 to 1
- cand_clip: int32 [2048], P('tile'), may hold values from 0 to 15
- cand_owner: int32 [2048], replicated, may hold values from 0 to 31, as said below
- cand_live: int32 [2048], replicated, may hold values from 0 to 1, as said below
- kernels: bfloat16 [32, 12, 64, 128], P('tile'), may hold values from -4 to 4
- weights: float32 [32, 12], P('tile'), may hold values from 0.05 to 0.5
- support_blocks: int32 [2], replicated, may hold values from 0 to 31, as said below
Outputs:
- intensity: bfloat16 [2048, 256, 256], P('tile', 'panel')
The draws below stay inside these ranges and needn't reach their ends.
Inputs may be any that keep to these rules, and one draw needn't show every extreme that they name: `cand_owner`: each layout owner's 64 entries name every litho owner exactly 2 times. `cand_live`: some litho owner has all of its entries from every layout owner marked 1. `support_blocks`: distinct and ascending; the last is always block 31.
All inputs are finite; a program needn't handle non-finite values.
Results may differ from the reference program's by a relative error of at most 0.013.
Values may be sent and summed in bfloat16 or wider, within the bound.
No kernel may reach another device: no remote copies, remote signals or barrier semaphores. Data moves between devices by JAX's collectives and lax.ppermute only.
A program may use at most 192 MiB of HBM per device.

```python
import math
import jax
import jax.numpy as jnp
from jax import lax

N = 1024
BLK = 32
SB = 2
OUT = 256
K = 12
HELD = 16
SLOT = 2
OWNERS = 32
LIST = 64
CAND = 2048
CLIPS = 512
S = 64
NB = 32


def owner_table(key):
    keys = jax.random.split(key, OWNERS)
    shuffled = jax.vmap(lambda single: jax.random.permutation(single, LIST))(keys)
    return (shuffled // SLOT).astype(jnp.int32)


def draw_cand_owner(key, part):
    table = owner_table(key)
    return table.reshape(-1)


def draw_cand_live(key, part):
    table = owner_table(key)
    key = jax.random.fold_in(key, 12)
    first, second, third = jax.random.split(key, 3)
    levels = jax.random.randint(first, (OWNERS,), 1, 5)
    busiest = jax.random.randint(second, (), 0, OWNERS)
    coins = jax.random.randint(third, (OWNERS, LIST), 0, 4)
    chosen = (coins < levels[table]) | (table == busiest)
    return chosen.astype(jnp.int32).reshape(-1)


def draw_support_blocks(key, part):
    key = jax.random.fold_in(key, 13)
    shuffled = jax.random.permutation(key, NB - 1).astype(jnp.int32)
    lower_blocks = jnp.sort(shuffled[:SB - 1]).astype(jnp.int32)
    last_block = jnp.full((1,), NB - 1, jnp.int32)
    return jnp.concatenate([lower_blocks, last_block]).astype(jnp.int32)


def plant(array, rng, least, high):
    longest = array.shape.index(max(array.shape))
    spots = []
    for shift in (0, 1):
        where = [jax.random.randint(jax.random.fold_in(rng, axis), (), 0, length) for axis, length in enumerate(array.shape)]
        where[longest] = (where[longest] + shift) % array.shape[longest]
        spots.append(tuple(where))
    return array.at[spots[0]].set(least).at[spots[1]].set(high)


def shard_levels(stream_key, shape, pieces, low, top_value):
    gain, own = 1.0, jax.random.fold_in(stream_key, 6)
    for position, parts in pieces:
        draws = jnp.exp(jax.random.uniform(jax.random.fold_in(own, position), (parts,), jnp.float32, low / len(pieces), top_value / len(pieces)))
        gain = gain * jnp.repeat(draws, shape[position] // parts).reshape([-1 if axis == position else 1 for axis in range(len(shape))])
    return gain


def gaussian(rng, dims, scale, most, pieces=(), kind=jnp.bfloat16):
    loudness = shard_levels(rng, dims, pieces, -0.22, 0.18) if pieces else 1.0
    array = jax.random.normal(rng, dims, jnp.float32) * scale * loudness
    return jnp.minimum(jnp.maximum(array, -most), most).astype(kind)


def setup_inputs(seed: int = 0) -> dict:
    arg_keys = jax.random.split(jax.random.key(seed), 8)
    return {
        "masks": jnp.clip(jax.random.uniform(arg_keys[0], (CLIPS, N, N), jnp.float32, -1.0, 1.0) * shard_levels(arg_keys[0], (CLIPS, N, N), ((0, 32), (1, 4)), -0.4, 0.0), -1.0, 1.0).astype(jnp.bfloat16),
        "cand_clip": plant(jax.random.randint(arg_keys[1], (CAND,), 0, HELD), jax.random.fold_in(arg_keys[1], 1), 0, HELD - 1).astype(jnp.int32),
        "cand_owner": draw_cand_owner(jax.random.fold_in(arg_keys[7], 71), 0),
        "cand_live": draw_cand_live(jax.random.fold_in(arg_keys[7], 71), 0),
        "kernels": gaussian(arg_keys[4], (OWNERS, K, S, 2 * S), 1.0, 4.0, ((0, 32),)),
        "weights": jnp.clip(jnp.exp(math.log(0.5) - 2.3025851 * jax.random.uniform(arg_keys[5], (OWNERS, K), jnp.float32) ** shard_levels(arg_keys[5], (OWNERS, K), ((0, 32),), -0.2, 0.2)), 0.05, 0.5),
        "support_blocks": draw_support_blocks(jax.random.fold_in(arg_keys[7], 71), 0),
    }


def tables(positions, freqs, pixels, factor):
    phase = (positions[:, None] * freqs[None, :]) % pixels
    angle = phase.astype(jnp.float32) * (2.0 * math.pi / pixels)
    return (jnp.cos(angle) * factor).astype(jnp.bfloat16), (jnp.sin(angle) * factor).astype(jnp.bfloat16)


def picture(spectrum, kernel_set, weight_set, live_flag, left_table, right_table):
    support = spectrum.shape[0]
    width = right_table.shape[1] // 2
    k_re = kernel_set[:, :, :support].astype(jnp.float32)
    k_im = kernel_set[:, :, support:].astype(jnp.float32)
    s_re = spectrum[None, :, :support]
    s_im = spectrum[None, :, support:]
    live_value = live_flag.astype(jnp.float32)
    field_re = (k_re * s_re - k_im * s_im) * live_value
    field_im = (k_re * s_im + k_im * s_re) * live_value
    field = jnp.concatenate([field_re, field_im], -1).astype(jnp.bfloat16)
    lowered = jnp.concatenate([-field[:, :, support:], field[:, :, :support]], -1)
    stacked = jnp.concatenate([field, lowered], 1)
    pupil_out = jnp.einsum('ua,kab->kub', left_table.astype(jnp.float32), stacked.astype(jnp.float32)).astype(jnp.bfloat16)
    kernel_count, image_rows = pupil_out.shape[0], pupil_out.shape[1]
    amplitude = jnp.dot(pupil_out.reshape(-1, 2 * support), right_table, preferred_element_type=jnp.float32)
    amplitude = amplitude.reshape(kernel_count, image_rows, 2 * width)
    power = amplitude[:, :, :width] ** 2 + amplitude[:, :, width:] ** 2
    return jnp.sum(weight_set[:, None, None] * power, 0).astype(jnp.bfloat16)


def reference(masks, cand_clip, cand_owner, cand_live, kernels, weights, support_blocks):
    freqs = (support_blocks[:, None] * BLK + jnp.arange(BLK, dtype=jnp.int32)[None, :]).reshape(-1).astype(jnp.int32)
    col_cos, col_sin = tables(jnp.arange(N, dtype=jnp.int32), freqs, N, N ** -0.5)
    img_cos, img_sin = tables(jnp.arange(OUT, dtype=jnp.int32) * (N // OUT), freqs, N, S ** -0.5)
    col_table = jnp.concatenate([col_cos, -col_sin], 1)
    row_left = jnp.concatenate([col_cos, col_sin], 0)

    def clip_spectrum(mask):
        column_part = jnp.dot(mask, col_table, preferred_element_type=jnp.float32).astype(jnp.bfloat16)
        swapped = jnp.concatenate([column_part[:, S:], -column_part[:, :S]], 1)
        return jnp.dot(row_left.T, jnp.concatenate([column_part, swapped], 0), preferred_element_type=jnp.float32)

    spectra = lax.map(clip_spectrum, masks)
    left_table = jnp.concatenate([img_cos, img_sin], 1)
    upper = jnp.concatenate([img_cos.T, img_sin.T], 1)
    lower = jnp.concatenate([-img_sin.T, img_cos.T], 1)
    right_table = jnp.concatenate([upper, lower], 0)
    global_clip = (jnp.arange(CAND, dtype=jnp.int32) // LIST) * HELD + cand_clip

    def candidate_image(entry):
        clip_index, owner_index, live_flag = entry
        return picture(spectra[clip_index], kernels[owner_index], weights[owner_index], live_flag, left_table, right_table)

    return lax.map(candidate_image, (global_clip.astype(jnp.int32), cand_owner, cand_live))
```

```python
import functools
import math

import jax
import jax.numpy as jnp
import numpy as np
from jax import lax
from jax.experimental import pallas as pl
from jax.experimental.pallas import tpu as pltpu
from jax.sharding import PartitionSpec as P

BLK = 32
OUT = 256
SIDE = 4
CORES = 2
OUT_SLOTS = 4
KERNEL_SLOTS = 3
GROUP = 16
F32 = jnp.float32
BF16 = jnp.bfloat16


def block_tables(pixels):
    phase = np.arange(pixels)[:, None] * np.arange(pixels)[None, :] % pixels
    angle = phase * (2.0 * math.pi / pixels)
    factor = pixels ** (-0.5)
    blocks = pixels // BLK
    cos = (np.cos(angle) * factor).reshape(pixels, blocks, BLK).transpose(1, 0, 2)
    sin = (np.sin(angle) * factor).reshape(pixels, blocks, BLK).transpose(1, 0, 2)
    gap = np.zeros_like(cos)
    return np.concatenate([cos, gap, -sin, gap], -1).astype(jnp.bfloat16)


def swap_halves(value):
    return pltpu.roll(value, value.shape[-1] // 2, value.ndim - 1)


def spectrum_body(
    place, masks, first, second, partial, left, right, whole, table, row_table
):
    pixels, lanes = table.shape
    mask_rows = masks.shape[1]
    image_rows = left.shape[0]
    half = lanes // 2
    stride = pixels // OUT

    @pl.when(pl.program_id(0) == 0)
    def _():
        whole[...] = first[0].astype(F32) + pltpu.roll(second[0].astype(F32), BLK, 1)
        table[...] = whole[...].astype(BF16)
        start = place[2] * mask_rows
        own = whole[pl.ds(pl.multiple_of(start, mask_rows), mask_rows), :]
        row_table[...] = own.T.astype(BF16)
        scale = math.sqrt(pixels / half)
        sign = jnp.where(lax.broadcasted_iota(jnp.int32, (image_rows, lanes), 1) < half, scale, -scale)
        own_image = whole[pl.ds(pl.multiple_of(start, mask_rows), image_rows, stride=stride), :]
        left[...] = (own_image * sign).astype(BF16)
        image = (whole[pl.ds(0, OUT, stride=stride), :] * scale).T
        right[:, :OUT] = image.astype(BF16)
        right[:half, OUT:] = (-image[half:]).astype(BF16)
        right[half:, OUT:] = image[:half].astype(BF16)

    count = masks.shape[0]
    columns = jnp.dot(
        masks[...].reshape(count * mask_rows, pixels), table[...], preferred_element_type=F32
    ).astype(BF16)
    sign = jnp.where(lax.broadcasted_iota(jnp.int32, (half, lanes), 1) < half, -1.0, 1.0)
    for clip in range(count):
        both = jnp.dot(
            row_table[...],
            columns[clip * mask_rows : (clip + 1) * mask_rows],
            preferred_element_type=F32,
        )
        partial[clip] = (both[:half] + swap_halves(both[half:]) * sign).astype(BF16)


def partial_spectra(masks, place, tables):
    held, mask_rows, pixels = masks.shape
    lanes = tables.shape[2]
    image_rows = mask_rows * OUT // pixels
    step = math.gcd(held, 2)
    return pl.pallas_call(
        spectrum_body,
        grid_spec=pltpu.PrefetchScalarGridSpec(
            num_scalar_prefetch=1,
            grid=(held // step,),
            in_specs=[
                pl.BlockSpec((step, mask_rows, pixels), lambda i, place: (i, 0, 0)),
                pl.BlockSpec((1, pixels, lanes), lambda i, place: (place[0], 0, 0)),
                pl.BlockSpec((1, pixels, lanes), lambda i, place: (place[1], 0, 0)),
            ],
            out_specs=[
                pl.BlockSpec((step, lanes // 2, lanes), lambda i, place: (i, 0, 0)),
                pl.BlockSpec((image_rows, lanes), lambda i, place: (0, 0)),
                pl.BlockSpec((lanes, 2 * OUT), lambda i, place: (0, 0)),
            ],
            scratch_shapes=[
                pltpu.VMEM((pixels, lanes), F32),
                pltpu.VMEM((pixels, lanes), BF16),
                pltpu.VMEM((lanes, mask_rows), BF16),
            ],
        ),
        out_shape=[
            jax.ShapeDtypeStruct((held, lanes // 2, lanes), BF16),
            jax.ShapeDtypeStruct((image_rows, lanes), BF16),
            jax.ShapeDtypeStruct((lanes, 2 * OUT), BF16),
        ],
        compiler_params=pltpu.CompilerParams(vmem_limit_bytes=32 << 20),
        cost_estimate=pl.CostEstimate(
            flops=2 * held * mask_rows * pixels * lanes,
            bytes_accessed=2 * held * mask_rows * pixels,
            transcendentals=0,
        ),
    )(place, masks, tables, tables)


def spread(spectrum):
    half = spectrum.shape[1] // 2
    low = lax.broadcasted_iota(jnp.int32, spectrum.shape, 1) < half
    other = swap_halves(spectrum)
    return (
        jnp.where(low, spectrum, other),
        jnp.where(low, -other, spectrum),
        jnp.where(low, -other, -spectrum),
        jnp.where(low, -spectrum, other),
    )


def first_product(kernel_set, factors, left, pupil):
    kernel_count = kernel_set.shape[0]
    rows = left.shape[0]
    lanes = kernel_set.shape[2]
    straight, crossed, lowered, lowered_crossed = factors
    columns = []
    for k in range(kernel_count):
        kernel = kernel_set[k].astype(F32)
        other = swap_halves(kernel)
        field = (kernel * straight + other * crossed).astype(BF16)
        below = (kernel * lowered + other * lowered_crossed).astype(BF16)
        columns.append(jnp.concatenate([field, below], 0))
    product = jnp.dot(left, jnp.concatenate(columns, 1), preferred_element_type=F32).astype(BF16)
    for k in range(kernel_count):
        pupil[k * rows : (k + 1) * rows, :] = product[:, k * lanes : (k + 1) * lanes]


def second_product(pupil, right, rows):
    amplitude = jnp.dot(pupil[...], right[...], preferred_element_type=F32)
    real, imag = amplitude[:, :OUT], amplitude[:, OUT:]
    power = real * real + imag * imag
    total = power[:rows]
    for k in range(1, power.shape[0] // rows):
        total = total + power[k * rows : (k + 1) * rows]
    return total.astype(BF16)


def imaging_body(group, sets, *refs):
    entries, near, far, left, right = refs[:5]
    sources = refs[5 : 5 + sets]
    images = refs[-9]
    held_kernels, even, odd, out_buffer, zeros, kernel_sems, out_sems, zero_sem = refs[-8:]
    base = group * GROUP
    rows = left.shape[0]
    per_set = sources[0].shape[0]

    live = lax.fori_loop(0, GROUP, lambda i, n: n + (entries[base + i] >> 13), jnp.int32(0))

    def place(e):
        return entries[base + e] & 63

    def fetch(e):
        slot = (entries[base + e] >> 6) & 7
        buffer = lax.rem(e, KERNEL_SLOTS)
        for which in range(sets):

            @pl.when((slot >= which * per_set) & (slot < (which + 1) * per_set))
            def _():
                pltpu.make_async_copy(
                    sources[which].at[slot - which * per_set],
                    held_kernels.at[buffer],
                    kernel_sems.at[buffer],
                ).start()

    def fetched(e):
        buffer = lax.rem(e, KERNEL_SLOTS)
        pltpu.make_async_copy(
            sources[0].at[0], held_kernels.at[buffer], kernel_sems.at[buffer]
        ).wait()
        return held_kernels.at[buffer]

    def put(e):
        buffer = lax.rem(e, OUT_SLOTS)
        return pltpu.make_async_copy(
            out_buffer.at[buffer], images.at[place(e)], out_sems.at[buffer]
        )

    def put_zeros(e):
        return pltpu.make_async_copy(zeros, images.at[place(e)], zero_sem)

    def factors(e):
        clip = (entries[base + e] >> 9) & 15
        return spread(near[clip].astype(F32) + far[clip].astype(F32))

    @pl.when(live < GROUP)
    def _():
        zeros[...] = jnp.zeros_like(zeros)
        lax.fori_loop(live, GROUP, lambda e, _: put_zeros(e).start(), None)

    @pl.when(live > 0)
    def _():
        fetch(0)

        @pl.when(live > 1)
        def _():
            fetch(1)

        first_product(fetched(0), factors(0), left[...], even)

    pupils = (even, odd)

    def pair(i, _):
        for parity in (0, 1):
            e = 2 * i + parity

            @pl.when(e + 2 < live)
            def _():
                fetch(e + 2)

            @pl.when((e >= OUT_SLOTS) & (e < live))
            def _():
                put(e - OUT_SLOTS).wait()

            @pl.when(e + 1 < live)
            def _():
                fetched(e + 1)

            ahead = jnp.minimum(e + 1, GROUP - 1)
            picture = second_product(pupils[parity], right, rows)
            first_product(
                held_kernels.at[lax.rem(e + 1, KERNEL_SLOTS)],
                factors(ahead),
                left[...],
                pupils[1 - parity],
            )

            @pl.when(e < live)
            def _():
                out_buffer[lax.rem(e, OUT_SLOTS)] = picture
                put(e).start()

    lax.fori_loop(0, (live + 1) // 2, pair, None)
    for back in range(1, OUT_SLOTS + 1):

        @pl.when(live >= back)
        def _():
            put(live - back).wait()

    lax.fori_loop(live, GROUP, lambda e, _: put_zeros(e).wait(), None)


def imaging(group, entries, near, far, left, right, sources, images):
    rows = left.shape[0]
    kernel_count, support, lanes = sources[0].shape[1:]
    in_vmem = pl.BlockSpec(memory_space=pltpu.VMEM)
    anywhere = pl.BlockSpec(memory_space=pl.ANY)
    listed = entries.shape[0]
    operands = [entries, near, far, left, right, *sources]
    specs = [pl.BlockSpec(memory_space=pltpu.SMEM)] + [in_vmem] * 4 + [anywhere] * len(sources)
    aliases = {}
    if images is not None:
        aliases = {len(operands): 0}
        operands.append(images)
        specs.append(anywhere)
    return pl.pallas_call(
        functools.partial(imaging_body, group, len(sources)),
        in_specs=specs,
        out_specs=anywhere,
        out_shape=jax.ShapeDtypeStruct((listed, rows, OUT), BF16),
        input_output_aliases=aliases,
        scratch_shapes=[
            pltpu.VMEM((KERNEL_SLOTS, kernel_count, support, lanes), BF16),
            pltpu.VMEM((kernel_count * rows, lanes), BF16),
            pltpu.VMEM((kernel_count * rows, lanes), BF16),
            pltpu.VMEM((OUT_SLOTS, rows, OUT), BF16),
            pltpu.VMEM((rows, OUT), BF16),
            pltpu.SemaphoreType.DMA((KERNEL_SLOTS,)),
            pltpu.SemaphoreType.DMA((OUT_SLOTS,)),
            pltpu.SemaphoreType.DMA,
        ],
        compiler_params=pltpu.CompilerParams(vmem_limit_bytes=32 << 20),
        cost_estimate=pl.CostEstimate(
            flops=2 * GROUP * kernel_count * rows * lanes * (lanes + 2 * OUT),
            bytes_accessed=GROUP * kernel_count * support * lanes * 4,
            transcendentals=0,
        ),
    )(*operands)


def tile_of(x, z, core):
    return (x * SIDE + z) * CORES + core


def partners(axes, flip):
    pairs = []
    for x in range(SIDE):
        for z in range(SIDE):
            for core in range(CORES):
                there = (x ^ flip, z) if axes[core] == "x" else (x, z ^ flip)
                pairs.append((tile_of(x, z, core), tile_of(*there, core)))
    return pairs


def entry_list(cand_clip, own_owner, own_live, tile_index):
    listed = cand_clip.shape[0]
    core = tile_index & 1
    other_core = own_owner & 1
    across_x = (own_owner >> 3) ^ (tile_index >> 3)
    across_z = ((own_owner >> 1) ^ (tile_index >> 1)) & 3
    first = jnp.where(other_core == 0, across_x, across_z)
    second = jnp.where(other_core == 0, across_z, across_x)
    in_b = first >> 1
    mixed = (second >> 1) ^ (second & 1)
    high = second >> 1
    later = jnp.where(in_b == 1, mixed, high)
    pair = jnp.where(in_b == 1, high, mixed)
    slot = in_b * 4 + pair * 2 + ((first & 1) ^ in_b)
    call = later * 2 + (other_core ^ core)
    index = jnp.arange(listed, dtype=jnp.int32)
    key = ((call * 2 + 1 - own_live) * 8 + slot) * listed + index
    rank = jnp.sum((key[:, None] < key[None, :]).astype(jnp.int32), 0)
    packed = index + slot * 64 + cand_clip * 512 + own_live * 8192
    return jnp.sum(jnp.where(rank[:, None] == index[None, :], packed[:, None], 0), 0)


def shards(masks, cand_clip, cand_owner, cand_live, kernels, weights, support_blocks):
    tile_index = lax.axis_index("tile")
    panel_index = lax.axis_index("panel")
    listed = cand_clip.shape[0]
    send = lambda value, axes, flip: lax.ppermute(value, "tile", partners(axes, flip))
    across = lambda value: lax.ppermute(
        value, "tile", [(i, i ^ 1) for i in range(SIDE * SIDE * CORES)]
    )
    panel = lambda value, flip: lax.ppermute(value, "panel", [(i, i ^ flip) for i in range(SIDE)])

    scaled = kernels.astype(F32) * jnp.sqrt(weights)[:, :, None, None]
    own = scaled.astype(BF16)
    one = send(own, "xz", 1)
    three = send(own, "xz", 3)
    two = send(one, "xz", 3)

    tables = jnp.asarray(block_tables(masks.shape[2]))
    place = jnp.concatenate([support_blocks, panel_index[None].astype(jnp.int32)])
    partial, left, right = partial_spectra(masks, place, tables)
    near = (partial.astype(F32) + panel(partial, 1).astype(F32)).astype(BF16)
    far = panel(near, 3)

    own_owner = lax.dynamic_slice_in_dim(cand_owner, tile_index * listed, listed)
    own_live = lax.dynamic_slice_in_dim(cand_live, tile_index * listed, listed)
    entries = entry_list(cand_clip, own_owner, own_live, tile_index)

    half_a = jnp.concatenate([own, one], 0)
    half_b = jnp.concatenate([three, two], 0)
    four_a = jnp.concatenate([half_a, send(half_a, "zx", 1)], 0)
    four_b = jnp.concatenate([half_b, send(half_b, "zx", 3)], 0)
    later_a = send(four_a, "zx", 3)
    later_b = send(four_b, "zx", 1)
    sibling_a, sibling_b = across(four_a), across(four_b)
    last_a, last_b = across(later_a), across(later_b)

    images = None
    calls = [(four_a, four_b), (sibling_a, sibling_b), (later_a, later_b), (last_a, last_b)]
    for group, sources in enumerate(calls):
        images = imaging(group, entries, near, far, left, right, sources, images)
    return images


def solution(mesh):
    return jax.shard_map(
        shards,
        mesh=mesh,
        in_specs=(
            P("tile", "panel", None),
            P("tile"),
            P(),
            P(),
            P("tile", None, None, None),
            P("tile", None),
            P(),
        ),
        out_specs=P("tile", "panel", None),
        check_vma=False,
    )
```

```python
import functools
import math

import jax
import jax.numpy as jnp
import numpy as np
from jax import lax
from jax.experimental import pallas as pl
from jax.experimental.pallas import tpu as pltpu
from jax.sharding import PartitionSpec as P

BLK = 32
OUT = 256
SIDE = 4
CORES = 2
OUT_SLOTS = 4
BATCH = 2
PACK = 16
CLIPS = 4
GROUP = 16
F32 = jnp.float32
BF16 = jnp.bfloat16


def block_tables(pixels):
    phase = np.arange(pixels)[:, None] * np.arange(pixels)[None, :] % pixels
    angle = phase * (2.0 * math.pi / pixels)
    factor = pixels ** (-0.5)
    blocks = pixels // BLK
    cos = (np.cos(angle) * factor).reshape(pixels, blocks, BLK).transpose(1, 0, 2)
    sin = (np.sin(angle) * factor).reshape(pixels, blocks, BLK).transpose(1, 0, 2)
    gap = np.zeros_like(cos)
    return np.concatenate([cos, gap, -sin, gap], -1).astype(jnp.bfloat16)


def swap_halves(value):
    return pltpu.roll(value, value.shape[-1] // 2, value.ndim - 1)


def spectrum_body(
    place, masks, tables, partial, left, right, blocks, whole, table, row_table, columns, block_sems
):
    pixels, lanes = table.shape
    held, mask_rows = masks.shape[:2]
    image_rows = left.shape[0]
    half = lanes // 2
    stride = pixels // OUT
    steps = held // CLIPS

    def load_block(which):
        return pltpu.make_async_copy(
            tables.at[place[which]], blocks.at[which], block_sems.at[which]
        )

    load_block(0).start()
    load_block(1).start()
    load_block(0).wait()
    load_block(1).wait()
    whole[...] = blocks[0].astype(F32) + pltpu.roll(blocks[1].astype(F32), BLK, 1)
    table[...] = whole[...].astype(BF16)
    start = pl.multiple_of(lax.axis_index("panel") * mask_rows, mask_rows)
    row_table[...] = whole[pl.ds(start, mask_rows), :].T.astype(BF16)
    flip = jnp.where(lax.broadcasted_iota(jnp.int32, (half, lanes), 1) < half, -1.0, 1.0)

    def row_transform(step):
        both = jnp.dot(row_table[...], columns[step % 2], preferred_element_type=F32)
        for clip in range(CLIPS):
            part = both[:, clip * lanes : (clip + 1) * lanes]
            partial[step * CLIPS + clip] = (part[:half] + swap_halves(part[half:]) * flip).astype(BF16)

    def image_tables():
        scale = math.sqrt(pixels / half)
        sign = jnp.where(lax.broadcasted_iota(jnp.int32, (image_rows, lanes), 1) < half, scale, -scale)
        left[...] = (whole[pl.ds(start, image_rows, stride=stride), :] * sign).astype(BF16)
        image = (whole[pl.ds(0, OUT, stride=stride), :] * scale).T
        right[:, :OUT] = image.astype(BF16)
        right[:half, OUT:] = (-image[half:]).astype(BF16)
        right[half:, OUT:] = image[:half].astype(BF16)

    for step in range(steps):
        product = jnp.dot(
            masks[step * CLIPS : (step + 1) * CLIPS].reshape(CLIPS * mask_rows, pixels),
            table[...],
            preferred_element_type=F32,
        ).astype(BF16)
        if step:
            row_transform(step - 1)
        for clip in range(CLIPS):
            columns[step % 2, :, clip * lanes : (clip + 1) * lanes] = product[
                clip * mask_rows : (clip + 1) * mask_rows
            ]
    row_transform(steps - 1)
    image_tables()


def partial_spectra(masks, place, tables):
    held, mask_rows, pixels = masks.shape
    lanes = tables.shape[2]
    image_rows = mask_rows * OUT // pixels
    in_hbm = pl.BlockSpec(memory_space=pltpu.HBM)
    in_vmem = pl.BlockSpec(memory_space=pltpu.VMEM)
    return pl.pallas_call(
        spectrum_body,
        in_specs=[pl.BlockSpec(memory_space=pltpu.SMEM), in_vmem, in_hbm],
        out_specs=[in_vmem] * 3,
        scratch_shapes=[
            pltpu.VMEM((2, pixels, lanes), BF16),
            pltpu.VMEM((pixels, lanes), F32),
            pltpu.VMEM((pixels, lanes), BF16),
            pltpu.VMEM((lanes, mask_rows), BF16),
            pltpu.VMEM((2, mask_rows, CLIPS * lanes), BF16),
            pltpu.SemaphoreType.DMA((2,)),
        ],
        out_shape=[
            jax.ShapeDtypeStruct((held, lanes // 2, lanes), BF16),
            jax.ShapeDtypeStruct((image_rows, lanes), BF16),
            jax.ShapeDtypeStruct((lanes, 2 * OUT), BF16),
        ],
        compiler_params=pltpu.CompilerParams(vmem_limit_bytes=40 << 20),
        cost_estimate=pl.CostEstimate(
            flops=2 * held * mask_rows * pixels * lanes,
            bytes_accessed=2 * held * mask_rows * pixels,
            transcendentals=0,
        ),
    )(place, masks, tables)


def spread(spectrum):
    half = spectrum.shape[1] // 2
    low = lax.broadcasted_iota(jnp.int32, spectrum.shape, 1) < half
    other = swap_halves(spectrum)
    return (
        jnp.where(low, spectrum, other),
        jnp.where(low, -other, spectrum),
        jnp.where(low, -1.0, 1.0).astype(BF16),
        None,
    )


def first_product(set_a, set_b, in_a, factors, left, pupil):
    kernel_count, _, lanes = set_a.shape
    rows = left.shape[0]
    straight, crossed, lowered, lowered_crossed = factors
    columns = []
    for k in range(kernel_count):
        kernel = jnp.where(in_a, set_a[k], set_b[k]).astype(F32)
        other = swap_halves(kernel)
        field = (kernel * straight + other * crossed).astype(BF16)
        below = swap_halves(field) * lowered
        columns.append(jnp.concatenate([field, below], 0))
    product = jnp.dot(left, jnp.concatenate(columns, 1), preferred_element_type=F32).astype(BF16)
    for part in range(rows // PACK):
        for k in range(kernel_count):
            start = (part * kernel_count + k) * PACK
            pupil[start : start + PACK, :] = product[
                part * PACK : (part + 1) * PACK, k * lanes : (k + 1) * lanes
            ]


def second_product(pupil, right, part, kernel_count):
    rows = kernel_count * PACK
    amplitude = jnp.dot(
        pupil[part * rows : (part + 1) * rows, :], right[...], preferred_element_type=F32
    )
    real, imag = amplitude[:, :OUT], amplitude[:, OUT:]
    power = real * real + imag * imag
    total = power[:PACK]
    for k in range(1, kernel_count):
        total = total + power[k * PACK : (k + 1) * PACK]
    return total.astype(BF16)


def imaging_body(group, aliased, *refs):
    entries, near, far, left, right, sets_a, sets_b = refs[:7]
    images = refs[7 + aliased]
    pupils, out_buffer, zeros, out_sems, zero_sem = refs[8 + aliased :]
    base = group * GROUP
    rows = left.shape[0]

    live = lax.fori_loop(0, GROUP, lambda i, n: n + (entries[base + i] >> 13), jnp.int32(0))

    def put(e):
        buffer = lax.rem(e, OUT_SLOTS)
        place = entries[base + e] & 63
        return pltpu.make_async_copy(out_buffer.at[buffer], images.at[place], out_sems.at[buffer])

    def put_zeros(e):
        return pltpu.make_async_copy(zeros, images.at[entries[base + e] & 63], zero_sem)

    def begin(e, pupil):
        entry = entries[base + jnp.minimum(e, GROUP - 1)]
        clip = (entry >> 9) & 15
        factors = spread(near[clip].astype(F32) + far[clip].astype(F32))
        slot = (entry >> 6) & 7
        place = slot & (sets_a.shape[0] - 1)
        in_a = slot < sets_a.shape[0]
        first_product(sets_a.at[place], sets_b.at[place], in_a, factors, left[...], pupil)

    @pl.when(live < GROUP)
    def _():
        zeros[...] = jnp.zeros_like(zeros)
        lax.fori_loop(live, GROUP, lambda e, _: put_zeros(e).start(), None)

    @pl.when(live > 0)
    def _():
        for b in range(BATCH):
            begin(b, pupils.at[0, b])

    def batch(i, _):
        e = i * BATCH
        for b in range(BATCH):

            @pl.when(e >= OUT_SLOTS)
            def _():
                put(e + b - OUT_SLOTS).wait()

        for side in (0, 1):

            @pl.when(lax.rem(i, 2) == side)
            def _():
                for b in range(BATCH):
                    buffer = lax.rem(e + b, OUT_SLOTS)
                    for part in range(rows // PACK):
                        out_buffer[buffer, part * PACK : (part + 1) * PACK, :] = second_product(
                            pupils.at[side, b], right, part, sets_a.shape[1]
                        )
                    begin(e + BATCH + b, pupils.at[1 - side, b])

        for b in range(BATCH):

            @pl.when(e + b < live)
            def _():
                put(e + b).start()

    batches = (live + BATCH - 1) // BATCH
    lax.fori_loop(0, batches, batch, None)
    waited = jnp.maximum(batches * BATCH - OUT_SLOTS, 0)
    lax.fori_loop(waited, live, lambda e, _: put(e).wait(), None)
    lax.fori_loop(live, GROUP, lambda e, _: put_zeros(e).wait(), None)


def imaging(group, entries, near, far, left, right, sets_a, sets_b, images):
    rows = left.shape[0]
    kernel_count, support, lanes = sets_a.shape[1:]
    in_vmem = pl.BlockSpec(memory_space=pltpu.VMEM)
    anywhere = pl.BlockSpec(memory_space=pl.ANY)
    listed = entries.shape[0]
    operands = [entries, near, far, left, right, sets_a, sets_b]
    specs = [pl.BlockSpec(memory_space=pltpu.SMEM)] + [in_vmem] * 6
    aliases = {}
    if images is not None:
        aliases = {len(operands): 0}
        operands.append(images)
        specs.append(anywhere)
    return pl.pallas_call(
        functools.partial(imaging_body, group, len(aliases)),
        in_specs=specs,
        out_specs=anywhere,
        out_shape=jax.ShapeDtypeStruct((listed, rows, OUT), BF16),
        input_output_aliases=aliases,
        scratch_shapes=[
            pltpu.VMEM((2, BATCH, kernel_count * rows, lanes), BF16),
            pltpu.VMEM((OUT_SLOTS, rows, OUT), BF16),
            pltpu.VMEM((rows, OUT), BF16),
            pltpu.SemaphoreType.DMA((OUT_SLOTS,)),
            pltpu.SemaphoreType.DMA,
        ],
        compiler_params=pltpu.CompilerParams(vmem_limit_bytes=32 << 20),
        cost_estimate=pl.CostEstimate(
            flops=2 * GROUP * kernel_count * rows * lanes * (lanes + 2 * OUT),
            bytes_accessed=GROUP * kernel_count * support * lanes * 2,
            transcendentals=0,
        ),
    )(*operands)


def tile_of(x, z, core):
    return (x * SIDE + z) * CORES + core


def partners(axes, flip):
    pairs = []
    for x in range(SIDE):
        for z in range(SIDE):
            for core in range(CORES):
                there = (x ^ flip, z) if axes[core] == "x" else (x, z ^ flip)
                pairs.append((tile_of(x, z, core), tile_of(*there, core)))
    return pairs


def entry_list(cand_clip, own_owner, own_live, tile_index):
    listed = cand_clip.shape[0]
    core = tile_index & 1
    other_core = own_owner & 1
    across_x = (own_owner >> 3) ^ (tile_index >> 3)
    across_z = ((own_owner >> 1) ^ (tile_index >> 1)) & 3
    first = jnp.where(other_core == 0, across_x, across_z)
    second = jnp.where(other_core == 0, across_z, across_x)
    in_b = first >> 1
    mixed = (second >> 1) ^ (second & 1)
    high = second >> 1
    later = jnp.where(in_b == 1, mixed, high)
    pair = jnp.where(in_b == 1, high, mixed)
    slot = in_b * 4 + pair * 2 + ((first & 1) ^ in_b)
    call = later * 2 + (other_core ^ core)
    index = jnp.arange(listed, dtype=jnp.int32)
    key = ((call * 2 + 1 - own_live) * 8 + slot) * listed + index
    rank = jnp.sum((key[:, None] < key[None, :]).astype(jnp.int32), 0)
    packed = index + slot * 64 + cand_clip * 512 + own_live * 8192
    return jnp.sum(jnp.where(rank[:, None] == index[None, :], packed[:, None], 0), 0)


def shards(masks, cand_clip, cand_owner, cand_live, kernels, weights, support_blocks):
    tile_index = lax.axis_index("tile")
    listed = cand_clip.shape[0]
    send = lambda value, axes, flip: lax.ppermute(value, "tile", partners(axes, flip))
    across = lambda value: lax.ppermute(
        value, "tile", [(i, i ^ 1) for i in range(SIDE * SIDE * CORES)]
    )
    panel = lambda value, flip: lax.ppermute(value, "panel", [(i, i ^ flip) for i in range(SIDE)])

    together = lambda *values: lax.optimization_barrier(values)

    own = (kernels.astype(F32) * jnp.sqrt(weights)[:, :, None, None]).astype(BF16)
    tables = jnp.asarray(block_tables(masks.shape[2]))
    one, three = send(own, "xz", 1), send(own, "xz", 3)
    partial, left, right = partial_spectra(masks, support_blocks, tables)
    one, three, partial = together(one, three, partial)

    two = send(one, "xz", 3)
    neighbour = panel(partial, 1)
    half_a = jnp.concatenate([own, one], 0)
    beyond_a = send(half_a, "zx", 1)
    own_owner = lax.dynamic_slice_in_dim(cand_owner, tile_index * listed, listed)
    own_live = lax.dynamic_slice_in_dim(cand_live, tile_index * listed, listed)
    entries = entry_list(cand_clip, own_owner, own_live, tile_index)
    two, neighbour, entries = together(two, neighbour, entries)

    near = (partial.astype(F32) + neighbour.astype(F32)).astype(BF16)
    far = panel(near, 3)
    half_b = jnp.concatenate([three, two], 0)
    beyond_b = send(half_b, "zx", 3)
    four_a = jnp.concatenate([half_a, beyond_a], 0)
    later_a, sibling_a = send(four_a, "zx", 3), across(four_a)
    beyond_b, far = together(beyond_b, far)
    four_b = jnp.concatenate([half_b, beyond_b], 0)
    later_b, sibling_b = send(four_b, "zx", 1), across(four_b)

    images = imaging(0, entries, near, far, left, right, four_a, four_b, None)
    images, sibling_a, sibling_b = together(images, sibling_a, sibling_b)
    images = imaging(1, entries, near, far, left, right, sibling_a, sibling_b, images)
    images, later_a, later_b = together(images, later_a, later_b)
    last_a, last_b = across(later_a), across(later_b)
    images = imaging(2, entries, near, far, left, right, later_a, later_b, images)
    images, last_a, last_b = together(images, last_a, last_b)
    images = imaging(3, entries, near, far, left, right, last_a, last_b, images)
    return images


def solution(mesh):
    return jax.shard_map(
        shards,
        mesh=mesh,
        in_specs=(
            P("tile", "panel", None),
            P("tile"),
            P(),
            P(),
            P("tile", None, None, None),
            P("tile", None),
            P(),
        ),
        out_specs=P("tile", "panel", None),
        check_vma=False,
    )
```

```python
import functools
import math

import jax
import jax.numpy as jnp
import numpy as np
from jax import lax
from jax.experimental import pallas as pl
from jax.experimental.pallas import tpu as pltpu
from jax.sharding import PartitionSpec as P

BLK = 32
OUT = 256
SIDE = 4
CORES = 2
OUT_SLOTS = 4
BATCH = 2
CHUNKS = 2
AHEAD = 2
PACK = 16
CLIPS = 4
GROUP = 16
F32 = jnp.float32
BF16 = jnp.bfloat16


def block_tables(pixels, panels):
    phase = np.arange(pixels)[:, None] * np.arange(pixels)[None, :] % pixels
    angle = phase * (2.0 * math.pi / pixels)
    blocks = pixels // BLK
    cos = np.cos(angle).reshape(pixels, blocks, BLK).transpose(1, 0, 2)
    sin = np.sin(angle).reshape(pixels, blocks, BLK).transpose(1, 0, 2)
    last_cos, last_sin = np.broadcast_to(cos[-1:], cos.shape), np.broadcast_to(sin[-1:], sin.shape)
    table = np.concatenate([cos, last_cos, -sin, -last_sin], -1)
    half = table.shape[-1] // 2
    column = table * pixels ** (-0.5)
    rows = column.reshape(blocks * panels, pixels // panels, 2 * half).transpose(0, 2, 1)
    image = table[:, :: pixels // OUT] * half ** (-0.5)
    left = np.concatenate([image[..., :half], -image[..., half:]], -1)
    left = left.reshape(blocks * panels, OUT // panels, 2 * half)
    left = np.pad(left, ((0, 0), (0, 0), (0, rows.shape[2] - 2 * half)))
    rows = np.concatenate([rows, left], 1)
    across = image.transpose(0, 2, 1)
    right = np.concatenate(
        [across, np.concatenate([-across[:, half:], across[:, :half]], 1)], -1
    )
    right = np.concatenate(np.split(right, right.shape[2] // (2 * half), 2), 1)
    column = np.concatenate([column, right], 1)
    return [jnp.asarray(value.astype(jnp.bfloat16)) for value in (column, rows)]


def swap_halves(value):
    return pltpu.roll(value, value.shape[-1] // 2, value.ndim - 1)


def spectrum_body(
    place, masks, tables, row_tables, low, high, left, right, held_masks, table, row_table, columns,
    mask_sems, table_sems,
):
    pixels, lanes = table.shape
    held, mask_rows = masks.shape[:2]
    half = lanes // 2
    steps = held // CLIPS
    chunk = held // CHUNKS
    block = place[0]
    here = block * (pixels // mask_rows) + lax.axis_index("panel")

    def load(part):
        which = pl.ds(part * chunk, chunk)
        return pltpu.make_async_copy(masks.at[which], held_masks.at[which], mask_sems.at[part])

    copies = [
        pltpu.make_async_copy(tables.at[block, pl.ds(0, pixels)], table, table_sems.at[0]),
        pltpu.make_async_copy(row_tables.at[here, pl.ds(0, lanes)], row_table, table_sems.at[1]),
        pltpu.make_async_copy(
            row_tables.at[here, pl.ds(lanes, left.shape[0]), pl.ds(0, lanes)], left, table_sems.at[2]
        ),
    ]
    for part in range(right.shape[1] // lanes):
        copies.append(
            pltpu.make_async_copy(
                tables.at[block, pl.ds(pixels + part * lanes, lanes)],
                right.at[:, pl.ds(part * lanes, lanes)],
                table_sems.at[3 + part],
            )
        )
    copies[0].start()
    load(0).start()
    for copy in copies[1:]:
        copy.start()
    for part in range(1, AHEAD):
        load(part).start()
    copies[0].wait()
    copies[1].wait()
    flip = jnp.where(lax.broadcasted_iota(jnp.int32, (half, lanes), 1) < half, -1.0, 1.0)

    def row_transform(step):
        both = jnp.dot(row_table[...], columns[step % 2], preferred_element_type=F32)
        for clip in range(CLIPS):
            part = both[:, clip * lanes : (clip + 1) * lanes]
            place = step * CLIPS + clip
            partial = low if place < held // 2 else high
            partial[place % (held // 2)] = (part[:half] + swap_halves(part[half:]) * flip).astype(BF16)

    for step in range(steps):
        if step * CLIPS % chunk == 0:
            part = step * CLIPS // chunk
            load(part).wait()
            if part + AHEAD < CHUNKS:
                load(part + AHEAD).start()
        product = jnp.dot(
            held_masks[step * CLIPS : (step + 1) * CLIPS].reshape(CLIPS * mask_rows, pixels),
            table[...],
            preferred_element_type=F32,
        ).astype(BF16)
        if step:
            row_transform(step - 1)
        for clip in range(CLIPS):
            columns[step % 2, :, clip * lanes : (clip + 1) * lanes] = product[
                clip * mask_rows : (clip + 1) * mask_rows
            ]
    row_transform(steps - 1)
    for copy in copies[2:]:
        copy.wait()


def partial_spectra(masks, place, tables):
    held, mask_rows, pixels = masks.shape
    lanes = tables[0].shape[2]
    image_rows = mask_rows * OUT // pixels
    anywhere = pl.BlockSpec(memory_space=pl.ANY)
    in_vmem = pl.BlockSpec(memory_space=pltpu.VMEM)
    return pl.pallas_call(
        spectrum_body,
        in_specs=[pl.BlockSpec(memory_space=pltpu.SMEM)] + [anywhere] * 3,
        out_specs=[in_vmem] * 4,
        scratch_shapes=[
            pltpu.VMEM((held, mask_rows, pixels), BF16),
            pltpu.VMEM((pixels, lanes), BF16),
            pltpu.VMEM((lanes, mask_rows), BF16),
            pltpu.VMEM((2, mask_rows, CLIPS * lanes), BF16),
            pltpu.SemaphoreType.DMA((CHUNKS,)),
            pltpu.SemaphoreType.DMA((3 + 2 * OUT // lanes,)),
        ],
        out_shape=[
            jax.ShapeDtypeStruct((held // 2, lanes // 2, lanes), BF16),
            jax.ShapeDtypeStruct((held // 2, lanes // 2, lanes), BF16),
            jax.ShapeDtypeStruct((image_rows, lanes), BF16),
            jax.ShapeDtypeStruct((lanes, 2 * OUT), BF16),
        ],
        compiler_params=pltpu.CompilerParams(vmem_limit_bytes=48 << 20),
        cost_estimate=pl.CostEstimate(
            flops=2 * held * mask_rows * pixels * lanes,
            bytes_accessed=2 * held * mask_rows * pixels,
            transcendentals=0,
        ),
    )(place, masks, *tables)


def spread(spectrum):
    half = spectrum.shape[1] // 2
    low = lax.broadcasted_iota(jnp.int32, spectrum.shape, 1) < half
    other = swap_halves(spectrum)
    return (
        jnp.where(low, spectrum, other),
        jnp.where(low, -other, spectrum),
        jnp.where(low, -1.0, 1.0).astype(BF16),
        None,
    )


def first_product(set_a, set_b, in_a, factors, left, pupil):
    kernel_count, _, lanes = set_a.shape
    rows = left.shape[0]
    straight, crossed, lowered, lowered_crossed = factors
    columns = []
    for k in range(kernel_count):
        kernel = jnp.where(in_a, set_a[k], set_b[k]).astype(F32)
        other = swap_halves(kernel)
        field = (kernel * straight + other * crossed).astype(BF16)
        below = swap_halves(field) * lowered
        columns.append(jnp.concatenate([field, below], 0))
    product = jnp.dot(left, jnp.concatenate(columns, 1), preferred_element_type=F32).astype(BF16)
    for part in range(rows // PACK):
        for k in range(kernel_count):
            start = (part * kernel_count + k) * PACK
            pupil[start : start + PACK, :] = product[
                part * PACK : (part + 1) * PACK, k * lanes : (k + 1) * lanes
            ]


def second_product(pupil, right, part, kernel_count):
    rows = kernel_count * PACK
    amplitude = jnp.dot(
        pupil[part * rows : (part + 1) * rows, :], right[...], preferred_element_type=F32
    )
    real, imag = amplitude[:, :OUT], amplitude[:, OUT:]
    power = real * real + imag * imag
    total = power[:PACK]
    for k in range(1, kernel_count):
        total = total + power[k * PACK : (k + 1) * PACK]
    return total.astype(BF16)


def imaging_body(group, aliased, *refs):
    entries, near, far, left, right, sets_a, sets_b = refs[:7]
    images = refs[7 + aliased]
    pupils, out_buffer, zeros, out_sems, zero_sem = refs[8 + aliased :]
    base = group * GROUP
    rows = left.shape[0]

    live = lax.fori_loop(0, GROUP, lambda i, n: n + (entries[base + i] >> 13), jnp.int32(0))

    def put(e):
        buffer = lax.rem(e, OUT_SLOTS)
        place = entries[base + e] & 63
        return pltpu.make_async_copy(out_buffer.at[buffer], images.at[place], out_sems.at[buffer])

    def put_zeros(e):
        return pltpu.make_async_copy(zeros, images.at[entries[base + e] & 63], zero_sem)

    def begin(e, pupil):
        entry = entries[base + jnp.minimum(e, GROUP - 1)]
        clip = (entry >> 9) & 15
        factors = spread(near[clip].astype(F32) + far[clip].astype(F32))
        slot = (entry >> 6) & 7
        place = slot & (sets_a.shape[0] - 1)
        in_a = slot < sets_a.shape[0]
        first_product(sets_a.at[place], sets_b.at[place], in_a, factors, left[...], pupil)

    @pl.when(live < GROUP)
    def _():
        zeros[...] = jnp.zeros_like(zeros)
        lax.fori_loop(live, GROUP, lambda e, _: put_zeros(e).start(), None)

    @pl.when(live > 0)
    def _():
        for b in range(BATCH):
            begin(b, pupils.at[0, b])

    def batch(i, _):
        e = i * BATCH
        for b in range(BATCH):

            @pl.when(e >= OUT_SLOTS)
            def _():
                put(e + b - OUT_SLOTS).wait()

        for side in (0, 1):

            @pl.when(lax.rem(i, 2) == side)
            def _():
                for b in range(BATCH):
                    buffer = lax.rem(e + b, OUT_SLOTS)
                    for part in range(rows // PACK):
                        out_buffer[buffer, part * PACK : (part + 1) * PACK, :] = second_product(
                            pupils.at[side, b], right, part, sets_a.shape[1]
                        )
                    begin(e + BATCH + b, pupils.at[1 - side, b])

        for b in range(BATCH):

            @pl.when(e + b < live)
            def _():
                put(e + b).start()

    batches = (live + BATCH - 1) // BATCH
    lax.fori_loop(0, batches, batch, None)
    waited = jnp.maximum(batches * BATCH - OUT_SLOTS, 0)
    lax.fori_loop(waited, live, lambda e, _: put(e).wait(), None)
    lax.fori_loop(live, GROUP, lambda e, _: put_zeros(e).wait(), None)


def imaging(group, entries, near, far, left, right, sets_a, sets_b, images):
    rows = left.shape[0]
    kernel_count, support, lanes = sets_a.shape[1:]
    in_vmem = pl.BlockSpec(memory_space=pltpu.VMEM)
    anywhere = pl.BlockSpec(memory_space=pl.ANY)
    listed = entries.shape[0]
    operands = [entries, near, far, left, right, sets_a, sets_b]
    specs = [pl.BlockSpec(memory_space=pltpu.SMEM)] + [in_vmem] * 6
    aliases = {}
    if images is not None:
        aliases = {len(operands): 0}
        operands.append(images)
        specs.append(anywhere)
    return pl.pallas_call(
        functools.partial(imaging_body, group, len(aliases)),
        in_specs=specs,
        out_specs=anywhere,
        out_shape=jax.ShapeDtypeStruct((listed, rows, OUT), BF16),
        input_output_aliases=aliases,
        scratch_shapes=[
            pltpu.VMEM((2, BATCH, kernel_count * rows, lanes), BF16),
            pltpu.VMEM((OUT_SLOTS, rows, OUT), BF16),
            pltpu.VMEM((rows, OUT), BF16),
            pltpu.SemaphoreType.DMA((OUT_SLOTS,)),
            pltpu.SemaphoreType.DMA,
        ],
        compiler_params=pltpu.CompilerParams(vmem_limit_bytes=32 << 20),
        cost_estimate=pl.CostEstimate(
            flops=2 * GROUP * kernel_count * rows * lanes * (lanes + 2 * OUT),
            bytes_accessed=GROUP * kernel_count * support * lanes * 2,
            transcendentals=0,
        ),
    )(*operands)


def tile_of(x, z, core):
    return (x * SIDE + z) * CORES + core


def partners(axes, flip):
    pairs = []
    for x in range(SIDE):
        for z in range(SIDE):
            for core in range(CORES):
                there = (x ^ flip, z) if axes[core] == "x" else (x, z ^ flip)
                pairs.append((tile_of(x, z, core), tile_of(*there, core)))
    return pairs


def entry_list(cand_clip, own_owner, own_live, tile_index):
    listed = cand_clip.shape[0]
    core = tile_index & 1
    other_core = own_owner & 1
    across_x = (own_owner >> 3) ^ (tile_index >> 3)
    across_z = ((own_owner >> 1) ^ (tile_index >> 1)) & 3
    first = jnp.where(other_core == 0, across_x, across_z)
    second = jnp.where(other_core == 0, across_z, across_x)
    in_b = first >> 1
    mixed = (second >> 1) ^ (second & 1)
    high = second >> 1
    later = jnp.where(in_b == 1, mixed, high)
    pair = jnp.where(in_b == 1, high, mixed)
    slot = in_b * 4 + pair * 2 + ((first & 1) ^ in_b)
    call = later * 2 + (other_core ^ core)
    index = jnp.arange(listed, dtype=jnp.int32)
    key = ((call * 2 + 1 - own_live) * 8 + slot) * listed + index
    rank = jnp.sum((key[:, None] < key[None, :]).astype(jnp.int32), 0)
    packed = index + slot * 64 + cand_clip * 512 + own_live * 8192
    return jnp.sum(jnp.where(rank[:, None] == index[None, :], packed[:, None], 0), 0)


def shards(masks, cand_clip, cand_owner, cand_live, kernels, weights, support_blocks):
    tile_index = lax.axis_index("tile")
    listed = cand_clip.shape[0]
    send = lambda value, axes, flip: lax.ppermute(value, "tile", partners(axes, flip))
    across = lambda value: lax.ppermute(
        value, "tile", [(i, i ^ 1) for i in range(SIDE * SIDE * CORES)]
    )
    panel = lambda value, flip: lax.ppermute(value, "panel", [(i, i ^ flip) for i in range(SIDE)])

    together = lambda *values: lax.optimization_barrier(values)

    own = (kernels.astype(F32) * jnp.sqrt(weights)[:, :, None, None]).astype(BF16)
    tables = block_tables(masks.shape[2], SIDE)
    one, three, two = send(own, "xz", 1), send(own, "xz", 3), send(own, "xz", 2)
    low, high, left, right = partial_spectra(masks, support_blocks, tables)
    one, three, two, low, high = together(one, three, two, low, high)

    neighbour_low, neighbour_high = panel(low, 1), panel(high, 3)
    half_a = jnp.concatenate([own, one], 0)
    half_b = jnp.concatenate([three, two], 0)
    beyond_a, beyond_b = send(half_a, "zx", 1), send(half_b, "zx", 3)

    sums = lambda mine, other: (mine.astype(F32) + other.astype(F32)).astype(BF16)
    near_low, near_high = sums(low, neighbour_low), sums(high, neighbour_high)
    near_low, near_high, cand_clip = together(near_low, near_high, cand_clip)
    far_low, far_high = panel(near_low, 3), panel(near_high, 1)
    own_owner = lax.dynamic_slice_in_dim(cand_owner, tile_index * listed, listed)
    own_live = lax.dynamic_slice_in_dim(cand_live, tile_index * listed, listed)
    entries = entry_list(cand_clip, own_owner, own_live, tile_index)
    beyond_a, beyond_b, far_low, far_high, entries = together(
        beyond_a, beyond_b, far_low, far_high, entries
    )
    four_a = jnp.concatenate([half_a, beyond_a], 0)
    four_b = jnp.concatenate([half_b, beyond_b], 0)
    later_a, sibling_a = send(four_a, "zx", 3), across(four_a)
    later_b, sibling_b = send(four_b, "zx", 1), across(four_b)
    near = jnp.concatenate([near_low, near_high], 0)
    far = jnp.concatenate([far_low, far_high], 0)

    images = imaging(0, entries, near, far, left, right, four_a, four_b, None)
    images, sibling_a, sibling_b = together(images, sibling_a, sibling_b)
    images = imaging(1, entries, near, far, left, right, sibling_a, sibling_b, images)
    images, later_a, later_b = together(images, later_a, later_b)
    last_a, last_b = across(later_a), across(later_b)
    images = imaging(2, entries, near, far, left, right, later_a, later_b, images)
    images, last_a, last_b = together(images, last_a, last_b)
    images = imaging(3, entries, near, far, left, right, last_a, last_b, images)
    return images


def solution(mesh):
    return jax.shard_map(
        shards,
        mesh=mesh,
        in_specs=(
            P("tile", "panel", None),
            P("tile"),
            P(),
            P(),
            P("tile", None, None, None),
            P("tile", None),
            P(),
        ),
        out_specs=P("tile", "panel", None),
        check_vma=False,
    )
```

```python
import functools
import math

import jax
import jax.numpy as jnp
import numpy as np
from jax import lax
from jax.experimental import pallas as pl
from jax.experimental.pallas import tpu as pltpu
from jax.sharding import PartitionSpec as P

BLK = 32
OUT = 256
SIDE = 4
CORES = 2
OUT_SLOTS = 4
BATCH = 2
CHUNKS = 2
AHEAD = 2
PACK = 16
CLIPS = 4
GROUP = 16
F32 = jnp.float32
BF16 = jnp.bfloat16


def block_tables(pixels, panels):
    phase = np.arange(pixels)[:, None] * np.arange(pixels)[None, :] % pixels
    angle = phase * (2.0 * math.pi / pixels)
    blocks = pixels // BLK
    cos = np.cos(angle).reshape(pixels, blocks, BLK).transpose(1, 0, 2)
    sin = np.sin(angle).reshape(pixels, blocks, BLK).transpose(1, 0, 2)
    last_cos, last_sin = np.broadcast_to(cos[-1:], cos.shape), np.broadcast_to(sin[-1:], sin.shape)
    table = np.concatenate([cos, last_cos, -sin, -last_sin], -1)
    half = table.shape[-1] // 2
    column = table * pixels ** (-0.5)
    rows = column.reshape(blocks * panels, pixels // panels, 2 * half).transpose(0, 2, 1)
    image = table[:, :: pixels // OUT] * half ** (-0.5)
    left = np.concatenate([image[..., :half], -image[..., half:]], -1)
    left = left.reshape(blocks * panels, OUT // panels, 2 * half)
    left = np.pad(left, ((0, 0), (0, 0), (0, rows.shape[2] - 2 * half)))
    rows = np.concatenate([rows, left], 1)
    across = image.transpose(0, 2, 1)
    right = np.concatenate(
        [across, np.concatenate([-across[:, half:], across[:, :half]], 1)], -1
    )
    right = np.concatenate(np.split(right, right.shape[2] // (2 * half), 2), 1)
    column = np.concatenate([column, right], 1)
    return [jnp.asarray(value.astype(jnp.bfloat16)) for value in (column, rows)]


def swap_halves(value):
    return pltpu.roll(value, value.shape[-1] // 2, value.ndim - 1)


def spectrum_body(
    place, masks, tables, row_tables, low, high, left, right, held_masks, table, row_table, columns,
    mask_sems, table_sems,
):
    pixels, lanes = table.shape
    held, mask_rows = masks.shape[:2]
    half = lanes // 2
    steps = held // CLIPS
    chunk = held // CHUNKS
    block = place[0]
    here = block * (pixels // mask_rows) + lax.axis_index("panel")

    def load(part):
        which = pl.ds(part * chunk, chunk)
        return pltpu.make_async_copy(masks.at[which], held_masks.at[which], mask_sems.at[part])

    copies = [
        pltpu.make_async_copy(tables.at[block, pl.ds(0, pixels)], table, table_sems.at[0]),
        pltpu.make_async_copy(row_tables.at[here, pl.ds(0, lanes)], row_table, table_sems.at[1]),
        pltpu.make_async_copy(
            row_tables.at[here, pl.ds(lanes, left.shape[0]), pl.ds(0, lanes)], left, table_sems.at[2]
        ),
    ]
    for part in range(right.shape[1] // lanes):
        copies.append(
            pltpu.make_async_copy(
                tables.at[block, pl.ds(pixels + part * lanes, lanes)],
                right.at[:, pl.ds(part * lanes, lanes)],
                table_sems.at[3 + part],
            )
        )
    copies[0].start()
    load(0).start()
    for copy in copies[1:]:
        copy.start()
    for part in range(1, AHEAD):
        load(part).start()
    copies[0].wait()
    copies[1].wait()
    flip = jnp.where(lax.broadcasted_iota(jnp.int32, (half, lanes), 1) < half, -1.0, 1.0)

    def row_transform(step):
        both = jnp.dot(row_table[...], columns[step % 2], preferred_element_type=F32)
        for clip in range(CLIPS):
            part = both[:, clip * lanes : (clip + 1) * lanes]
            place = step * CLIPS + clip
            partial = low if place < held // 2 else high
            partial[place % (held // 2)] = (part[:half] + swap_halves(part[half:]) * flip).astype(BF16)

    for step in range(steps):
        if step * CLIPS % chunk == 0:
            part = step * CLIPS // chunk
            load(part).wait()
            if part + AHEAD < CHUNKS:
                load(part + AHEAD).start()
        product = jnp.dot(
            held_masks[step * CLIPS : (step + 1) * CLIPS].reshape(CLIPS * mask_rows, pixels),
            table[...],
            preferred_element_type=F32,
        ).astype(BF16)
        if step:
            row_transform(step - 1)
        for clip in range(CLIPS):
            columns[step % 2, :, clip * lanes : (clip + 1) * lanes] = product[
                clip * mask_rows : (clip + 1) * mask_rows
            ]
    row_transform(steps - 1)
    for copy in copies[2:]:
        copy.wait()


def partial_spectra(masks, place, tables):
    held, mask_rows, pixels = masks.shape
    lanes = tables[0].shape[2]
    image_rows = mask_rows * OUT // pixels
    anywhere = pl.BlockSpec(memory_space=pl.ANY)
    in_vmem = pl.BlockSpec(memory_space=pltpu.VMEM)
    return pl.pallas_call(
        spectrum_body,
        in_specs=[pl.BlockSpec(memory_space=pltpu.SMEM)] + [anywhere] * 3,
        out_specs=[in_vmem] * 4,
        scratch_shapes=[
            pltpu.VMEM((held, mask_rows, pixels), BF16),
            pltpu.VMEM((pixels, lanes), BF16),
            pltpu.VMEM((lanes, mask_rows), BF16),
            pltpu.VMEM((2, mask_rows, CLIPS * lanes), BF16),
            pltpu.SemaphoreType.DMA((CHUNKS,)),
            pltpu.SemaphoreType.DMA((3 + 2 * OUT // lanes,)),
        ],
        out_shape=[
            jax.ShapeDtypeStruct((held // 2, lanes // 2, lanes), BF16),
            jax.ShapeDtypeStruct((held // 2, lanes // 2, lanes), BF16),
            jax.ShapeDtypeStruct((image_rows, lanes), BF16),
            jax.ShapeDtypeStruct((lanes, 2 * OUT), BF16),
        ],
        compiler_params=pltpu.CompilerParams(vmem_limit_bytes=48 << 20),
        cost_estimate=pl.CostEstimate(
            flops=2 * held * mask_rows * pixels * lanes,
            bytes_accessed=2 * held * mask_rows * pixels,
            transcendentals=0,
        ),
    )(place, masks, *tables)


def spread(spectrum):
    half = spectrum.shape[1] // 2
    low = lax.broadcasted_iota(jnp.int32, spectrum.shape, 1) < half
    other = swap_halves(spectrum)
    return (
        jnp.where(low, spectrum, other),
        jnp.where(low, -other, spectrum),
        jnp.where(low, -1.0, 1.0).astype(BF16),
        None,
    )


def first_product(sets, which, factors, left, pupil):
    kernel_count, _, lanes = sets[0].shape
    rows = left.shape[0]
    straight, crossed, lowered, lowered_crossed = factors
    columns = []
    for k in range(kernel_count):
        kernel = sets[0][k]
        for other in range(1, len(sets)):
            kernel = jnp.where(which == other, sets[other][k], kernel)
        kernel = kernel.astype(F32)
        other = swap_halves(kernel)
        field = (kernel * straight + other * crossed).astype(BF16)
        below = swap_halves(field) * lowered
        columns.append(jnp.concatenate([field, below], 0))
    product = jnp.dot(left, jnp.concatenate(columns, 1), preferred_element_type=F32).astype(BF16)
    for part in range(rows // PACK):
        for k in range(kernel_count):
            start = (part * kernel_count + k) * PACK
            pupil[start : start + PACK, :] = product[
                part * PACK : (part + 1) * PACK, k * lanes : (k + 1) * lanes
            ]


def second_product(pupil, right, part, kernel_count):
    rows = kernel_count * PACK
    amplitude = jnp.dot(
        pupil[part * rows : (part + 1) * rows, :], right[...], preferred_element_type=F32
    )
    real, imag = amplitude[:, :OUT], amplitude[:, OUT:]
    power = real * real + imag * imag
    total = power[:PACK]
    for k in range(1, kernel_count):
        total = total + power[k * PACK : (k + 1) * PACK]
    return total.astype(BF16)


def imaging_body(base, count, sources, aliased, *refs):
    entries, near, far, left, right = refs[:5]
    sets = refs[5 : 5 + sources]
    images = refs[5 + sources + aliased]
    pupils, out_buffer, zeros, out_sems, zero_sem = refs[6 + sources + aliased :]
    rows = left.shape[0]

    live = lax.fori_loop(0, count, lambda i, n: n + (entries[base + i] >> 14), jnp.int32(0))

    def put(e):
        buffer = lax.rem(e, OUT_SLOTS)
        place = entries[base + e] & 63
        return pltpu.make_async_copy(out_buffer.at[buffer], images.at[place], out_sems.at[buffer])

    def put_zeros(e):
        return pltpu.make_async_copy(zeros, images.at[entries[base + e] & 63], zero_sem)

    def begin(e, pupil):
        entry = entries[base + jnp.minimum(e, count - 1)]
        clip = (entry >> 10) & 15
        factors = spread(near[clip].astype(F32) + far[clip].astype(F32))
        slot = (entry >> 6) & 15
        place = lax.rem(slot, sets[0].shape[0])
        which = slot // sets[0].shape[0]
        first_product([held.at[place] for held in sets], which, factors, left[...], pupil)

    @pl.when(live < count)
    def _():
        zeros[...] = jnp.zeros_like(zeros)
        lax.fori_loop(live, count, lambda e, _: put_zeros(e).start(), None)

    @pl.when(live > 0)
    def _():
        for b in range(BATCH):
            begin(b, pupils.at[0, b])

    def batch(i, _):
        e = i * BATCH
        for b in range(BATCH):

            @pl.when(e >= OUT_SLOTS)
            def _():
                put(e + b - OUT_SLOTS).wait()

        for side in (0, 1):

            @pl.when(lax.rem(i, 2) == side)
            def _():
                for b in range(BATCH):
                    buffer = lax.rem(e + b, OUT_SLOTS)
                    for part in range(rows // PACK):
                        out_buffer[buffer, part * PACK : (part + 1) * PACK, :] = second_product(
                            pupils.at[side, b], right, part, sets[0].shape[1]
                        )
                    begin(e + BATCH + b, pupils.at[1 - side, b])

        for b in range(BATCH):

            @pl.when(e + b < live)
            def _():
                put(e + b).start()

    batches = (live + BATCH - 1) // BATCH
    lax.fori_loop(0, batches, batch, None)
    waited = jnp.maximum(batches * BATCH - OUT_SLOTS, 0)
    lax.fori_loop(waited, live, lambda e, _: put(e).wait(), None)
    lax.fori_loop(live, count, lambda e, _: put_zeros(e).wait(), None)


def imaging(base, count, entries, near, far, left, right, sets, images):
    rows = left.shape[0]
    kernel_count, support, lanes = sets[0].shape[1:]
    in_vmem = pl.BlockSpec(memory_space=pltpu.VMEM)
    anywhere = pl.BlockSpec(memory_space=pl.ANY)
    listed = entries.shape[0]
    operands = [entries, near, far, left, right, *sets]
    specs = [pl.BlockSpec(memory_space=pltpu.SMEM)] + [in_vmem] * (4 + len(sets))
    aliases = {}
    if images is not None:
        aliases = {len(operands): 0}
        operands.append(images)
        specs.append(anywhere)
    return pl.pallas_call(
        functools.partial(imaging_body, base, count, len(sets), len(aliases)),
        in_specs=specs,
        out_specs=anywhere,
        out_shape=jax.ShapeDtypeStruct((listed, rows, OUT), BF16),
        input_output_aliases=aliases,
        scratch_shapes=[
            pltpu.VMEM((2, BATCH, kernel_count * rows, lanes), BF16),
            pltpu.VMEM((OUT_SLOTS, rows, OUT), BF16),
            pltpu.VMEM((rows, OUT), BF16),
            pltpu.SemaphoreType.DMA((OUT_SLOTS,)),
            pltpu.SemaphoreType.DMA,
        ],
        compiler_params=pltpu.CompilerParams(vmem_limit_bytes=32 << 20),
        cost_estimate=pl.CostEstimate(
            flops=2 * count * kernel_count * rows * lanes * (lanes + 2 * OUT),
            bytes_accessed=count * kernel_count * support * lanes * 2,
            transcendentals=0,
        ),
    )(*operands)


def tile_of(x, z, core):
    return (x * SIDE + z) * CORES + core


def partners(axes, flip):
    pairs = []
    for x in range(SIDE):
        for z in range(SIDE):
            for core in range(CORES):
                there = (x ^ flip, z) if axes[core] == "x" else (x, z ^ flip)
                pairs.append((tile_of(x, z, core), tile_of(*there, core)))
    return pairs


def entry_list(cand_clip, own_owner, own_live, tile_index):
    listed = cand_clip.shape[0]
    core = tile_index & 1
    other_core = own_owner & 1
    across_x = (own_owner >> 3) ^ (tile_index >> 3)
    across_z = ((own_owner >> 1) ^ (tile_index >> 1)) & 3
    first = jnp.where(other_core == 0, across_x, across_z)
    second = jnp.where(other_core == 0, across_z, across_x)
    in_b = first >> 1
    mixed = (second >> 1) ^ (second & 1)
    high = second >> 1
    later = jnp.where(in_b == 1, mixed, high)
    pair = jnp.where(in_b == 1, high, mixed)
    slot = in_b * 4 + pair * 2 + ((first & 1) ^ in_b)
    across_core = other_core ^ core
    call = later * (1 + across_core)
    slot = slot + 8 * across_core * (1 - later)
    index = jnp.arange(listed, dtype=jnp.int32)
    key = ((call * 2 + 1 - own_live) * 16 + slot) * listed + index
    rank = jnp.sum((key[:, None] < key[None, :]).astype(jnp.int32), 0)
    packed = index + slot * 64 + cand_clip * 1024 + own_live * 16384
    return jnp.sum(jnp.where(rank[:, None] == index[None, :], packed[:, None], 0), 0)


def shards(masks, cand_clip, cand_owner, cand_live, kernels, weights, support_blocks):
    tile_index = lax.axis_index("tile")
    listed = cand_clip.shape[0]
    send = lambda value, axes, flip: lax.ppermute(value, "tile", partners(axes, flip))
    across = lambda value: lax.ppermute(
        value, "tile", [(i, i ^ 1) for i in range(SIDE * SIDE * CORES)]
    )
    panel = lambda value, flip: lax.ppermute(value, "panel", [(i, i ^ flip) for i in range(SIDE)])

    together = lambda *values: lax.optimization_barrier(values)

    own = (kernels.astype(F32) * jnp.sqrt(weights)[:, :, None, None]).astype(BF16)
    tables = block_tables(masks.shape[2], SIDE)
    one, three, two = send(own, "xz", 1), send(own, "xz", 3), send(own, "xz", 2)
    low, high, left, right = partial_spectra(masks, support_blocks, tables)
    one, three, two, low, high = together(one, three, two, low, high)

    neighbour_low, neighbour_high = panel(low, 1), panel(high, 3)
    half_a = jnp.concatenate([own, one], 0)
    half_b = jnp.concatenate([three, two], 0)
    beyond_a, beyond_b = send(half_a, "zx", 1), send(half_b, "zx", 3)

    sums = lambda mine, other: (mine.astype(F32) + other.astype(F32)).astype(BF16)
    near_low, near_high = sums(low, neighbour_low), sums(high, neighbour_high)
    near_low, near_high, cand_clip = together(near_low, near_high, cand_clip)
    far_low, far_high = panel(near_low, 3), panel(near_high, 1)
    own_owner = lax.dynamic_slice_in_dim(cand_owner, tile_index * listed, listed)
    own_live = lax.dynamic_slice_in_dim(cand_live, tile_index * listed, listed)
    entries = entry_list(cand_clip, own_owner, own_live, tile_index)
    beyond_a, beyond_b, far_low, far_high, entries = together(
        beyond_a, beyond_b, far_low, far_high, entries
    )
    four_a = jnp.concatenate([half_a, beyond_a], 0)
    four_b = jnp.concatenate([half_b, beyond_b], 0)
    later_a, later_b = send(four_a, "zx", 3), send(four_b, "zx", 1)
    eight = jnp.concatenate([four_a, four_b], 0)
    sibling = across(eight)
    near = jnp.concatenate([near_low, near_high], 0)
    far = jnp.concatenate([far_low, far_high], 0)

    image = lambda base, count, sets, images: imaging(
        base, count, entries, near, far, left, right, sets, images
    )
    images = image(0, 2 * GROUP, (eight, sibling), None)
    images, later_a, later_b = together(images, later_a, later_b)
    later = jnp.concatenate([later_a, later_b], 0)
    last = across(later)
    images = image(2 * GROUP, GROUP, (later,), images)
    images, last = together(images, last)
    images = image(3 * GROUP, GROUP, (last,), images)
    return images


def solution(mesh):
    return jax.shard_map(
        shards,
        mesh=mesh,
        in_specs=(
            P("tile", "panel", None),
            P("tile"),
            P(),
            P(),
            P("tile", None, None, None),
            P("tile", None),
            P(),
        ),
        out_specs=P("tile", "panel", None),
        check_vma=False,
    )
```
